128 devices in a mesh: prow: 16 (over y, x_hi, core), pcol: 8 (over z, x_lo).
Axes of the slice: x: 4 (x_hi: 2, x_lo: 2; x = x_hi * 2 + x_lo), y: 4, z: 4, core: 2. Of those that a mesh axis runs over, the one named last changes fastest.
Arguments:
- sigma_anc: bfloat16 [8192, 8192], P('prow', 'pcol'), as said below
- lower_blocks: bfloat16 [32, 16, 256, 256], P('pcol', None, 'prow'), may hold values from -0.09375 to 0.09375
- row_blocks: int32 [32, 16], replicated, may hold values from 0 to 31, as said below
- slot_of: int32 [32], replicated, may hold values from 0 to 31, each once
- inv_diag: float32 [32, 256, 256], P('pcol', 'prow'), as said below
Outputs:
- sigma_off: bfloat16 [8192, 8192], P('prow', 'pcol')
- sigma_diag: float32 [32, 256, 256], P('pcol', 'prow')
The draws below stay inside these ranges and needn't reach their ends.
Inputs may be any that keep to these rules, and one draw needn't show every extreme that they name: `row_blocks`: each row holds 16 distinct ancestor indices in increasing order. `sigma_anc`: symmetric. `inv_diag`: symmetric.
All inputs are finite; a program needn't handle non-finite values.
Results may differ from the reference program's by a relative error of at most 0.015.
Values may be sent and summed in bfloat16 or wider, within the bound.
No kernel may reach another device: no remote copies, remote signals or barrier semaphores. Data moves between devices by JAX's collectives and lax.ppermute only.
A program may use at most 128 MiB of HBM per device.

```python
import math
import jax
import jax.numpy as jnp
from jax import lax

B = 256
NA = 32
NR = 16
NSUP = 32


def draw_sigma_anc(key, part):
    key = jax.random.fold_in(key, 11)
    order = NA * B
    base = jax.random.normal(key, (order, order), jnp.float32)
    shaped = (base + base.T) * 0.7071
    return shaped.astype(jnp.bfloat16)


def draw_row_blocks(key, part):
    key = jax.random.fold_in(key, 12)
    keys = jax.random.split(key, NSUP)
    rows = jax.vmap(lambda single: jnp.sort(jax.random.permutation(single, NA)[:NR]))(keys)
    return rows.astype(jnp.int32)


def draw_inv_diag(key, part):
    key = jax.random.fold_in(key, 13)
    base = jax.random.normal(key, (NSUP, B, B), jnp.float32)
    sym = (base + jnp.swapaxes(base, 1, 2)) * (0.5 / math.sqrt(B))
    lifted = jax.random.uniform(jax.random.fold_in(key, 1), (NSUP, B), jnp.float32, 1.0, 3.0)
    eye = jnp.eye(B, dtype=jnp.float32)
    return sym + lifted[:, :, None] * eye[None, :, :]


def levels(key, shape, pieces, least, top_value):
    def one(position, blocks):
        draws = jax.random.uniform(jax.random.fold_in(jax.random.fold_in(key, 6), position), (blocks,), jnp.float32, least / len(pieces), top_value / len(pieces))
        return jnp.repeat(jnp.exp(draws), shape[position] // blocks).reshape((-1,) + (1,) * (len(shape) - position - 1))

    level = one(*pieces[0])
    for cut in pieces[1:]:
        level = level * one(*cut)
    return level


def centred(stream_key, dims, width, most, pieces=(), kind=jnp.bfloat16):
    array = jax.random.normal(stream_key, dims, jnp.float32) * width
    if len(pieces) > 0:
        array = levels(stream_key, dims, pieces, -0.22, 0.18) * array
    return jnp.clip(array, min=-most, max=most).astype(kind)


def setup_inputs(seed: int = 0) -> dict:
    splits = jax.random.split(jax.random.key(seed), 6)
    return {
        "sigma_anc": draw_sigma_anc(jax.random.fold_in(splits[5], 71), 0),
        "lower_blocks": centred(splits[1], (NSUP, NR, B, B), (NR * B) ** -0.5, 0.09375, ((0, 8), (2, 16))),
        "row_blocks": draw_row_blocks(jax.random.fold_in(splits[5], 71), 0),
        "slot_of": jax.random.permutation(splits[3], NA).astype(jnp.int32),
        "inv_diag": draw_inv_diag(jax.random.fold_in(splits[5], 71), 0),
    }


def reference(sigma_anc, lower_blocks, row_blocks, slot_of, inv_diag):
    whole = sigma_anc.astype(jnp.float32)
    order = jnp.arange(NA, dtype=jnp.int32)
    slots = jnp.sum(jnp.where(row_blocks[:, :, None] == order[None, None, :], slot_of[None, None, :], 0), axis=2).astype(jnp.int32)
    onehot = (slots[:, :, None] == order[None, None, :]).astype(jnp.float32)
    live = jnp.sum(onehot, axis=1)

    def one_node(items):
        picks, blocks, alive, dinv = items
        panel = jnp.einsum("ca,cij->aij", picks, blocks.astype(jnp.float32), precision=lax.Precision.HIGHEST).reshape(NA * B, B)
        product = jnp.dot(whole, panel, precision=lax.Precision.HIGHEST)
        offdiag = (-(product.reshape(NA, B, B)) * alive[:, None, None]).astype(jnp.bfloat16).reshape(NA * B, B)
        quad = jnp.dot(panel.T, offdiag.astype(jnp.float32), precision=lax.Precision.HIGHEST)
        return offdiag, dinv - 0.5 * (quad + quad.T)

    offs, diags = lax.map(one_node, (onehot, lower_blocks, live, inv_diag))
    sigma_off = jnp.transpose(offs, (1, 0, 2)).reshape(NA * B, NSUP * B)
    return sigma_off, diags
```

```python
import jax
import jax.numpy as jnp
from jax import lax
from jax.experimental import pallas as pl
from jax.experimental.pallas import tpu as pltpu
from jax.sharding import PartitionSpec as P

B = 256
NR = 16
SUP = 4
NA = 32
VMEM_LIMIT = 48 * 1024 * 1024


def row_perm(fn):
    pairs = []
    for y in range(4):
        for h in range(2):
            for co in range(2):
                ty, th, tc = fn(y, h, co)
                pairs.append((y * 4 + h * 2 + co, (ty % 4) * 4 + (th % 2) * 2 + tc % 2))
    return pairs


def col_perm(fn):
    pairs = []
    for z in range(4):
        for w in range(2):
            tz, tw = fn(z, w)
            pairs.append((z * 2 + w, (tz % 4) * 2 + tw % 2))
    return pairs


def move_y(x, step):
    return lax.ppermute(x, "prow", row_perm(lambda y, h, co: (y + step, h, co)))


def swap_h(x):
    return lax.ppermute(x, "prow", row_perm(lambda y, h, co: (y, h + 1, co)))


def swap_core(x):
    return lax.ppermute(x, "prow", row_perm(lambda y, h, co: (y, h, co + 1)))


def move_z(x, step):
    return lax.ppermute(x, "pcol", col_perm(lambda z, w: (z + step, w)))


def swap_w(x):
    return lax.ppermute(x, "pcol", col_perm(lambda z, w: (z, w + 1)))


def first_kernel(inv_ref, place_ref, s0, s1, s2, s3, s4, s5, a0, a1, a2, a3, b0, b1, b2, b3,
                 acc_out, l_out, sv, lv, acc, s_sem, l_sem, o_sem):
    loads = []
    for p, src in enumerate((s0, s1, s2, s3, s4, s5)):
        for j in range(4):
            n = p * 4 + j
            loads.append(pltpu.make_async_copy(src.at[:, pl.ds(j * B, B)], sv.at[n], s_sem.at[n]))
    n = 0
    for part in (a0, a1, a2, a3, b0, b1, b2, b3):
        for h in range(2):
            row = pl.multiple_of(place_ref[n], 16)
            loads.append(pltpu.make_async_copy(part.at[h], lv.at[:, :, pl.ds(row, 16), :], l_sem.at[n]))
            n += 1
    for load in loads:
        load.start()
    acc[...] = jnp.zeros_like(acc)
    for load in loads:
        load.wait()
    keep = pltpu.make_async_copy(lv, l_out, o_sem.at[0])
    keep.start()

    def step(pos, carry):
        for k in range(SUP):
            c = inv_ref[k, pos]

            @pl.when(c >= 0)
            def _():
                acc[k] += jnp.dot(sv[pos], lv[k, c], preferred_element_type=jnp.float32)
        return carry

    lax.fori_loop(0, 24, step, 0)
    done = pltpu.make_async_copy(acc, acc_out, o_sem.at[1])
    done.start()
    done.wait()
    keep.wait()


def last_kernel(inv_ref, own_ref, core_ref, up, down, acc_in, l_in, off_out, keep_out, send_out,
                sv, lv, acc, tq, s_sem, l_sem):
    loads = []
    for p in range(2):
        for j in range(4):
            n = p * 4 + j
            loads.append(pltpu.make_async_copy(up.at[p, :, pl.ds(j * B, B)], sv.at[n, pl.ds(0, B)], s_sem.at[2 * n]))
            loads.append(pltpu.make_async_copy(down.at[p, :, pl.ds(j * B, B)], sv.at[n, pl.ds(B, B)], s_sem.at[2 * n + 1]))
    loads.append(pltpu.make_async_copy(acc_in, acc, l_sem.at[0]))
    loads.append(pltpu.make_async_copy(l_in, lv, l_sem.at[1]))
    for load in loads:
        load.start()
    for load in loads:
        load.wait()

    def step(pos, carry):
        for k in range(SUP):
            c = inv_ref[k, pos + 24]

            @pl.when(c >= 0)
            def _():
                acc[k] += jnp.dot(sv[pos], lv[k, c], preferred_element_type=jnp.float32)
        return carry

    lax.fori_loop(0, 8, step, 0)
    core = core_ref[0]
    for k in range(SUP):
        tq[...] = jnp.zeros_like(tq)
        for t in range(2):
            c = own_ref[k, t]

            @pl.when(c >= 0)
            def _():
                off = (-acc[k, pl.ds(t * B, B)]).astype(jnp.bfloat16)
                off_out[pl.ds(t * B, B), pl.ds(k * B, B)] = off
                tq[...] += lax.dot_general(lv[k, c], off, (((0,), (0,)), ((), ())),
                                           preferred_element_type=jnp.float32)

            @pl.when(c < 0)
            def _():
                off_out[pl.ds(t * B, B), pl.ds(k * B, B)] = jnp.zeros((B, B), jnp.bfloat16)
        total = tq[...]
        tq[...] = 0.5 * (total + total.T)
        for g in range(8):
            mine = pl.multiple_of((g * 2 + core) * 16, 16)
            other = pl.multiple_of((g * 2 + 1 - core) * 16, 16)
            keep_out[k, g] = tq[pl.ds(mine, 16), :]
            send_out[k, g] = tq[pl.ds(other, 16), :].astype(jnp.bfloat16)


def per_device(sigma_anc, lower_blocks, row_blocks, slot_of, inv_diag):
    row = lax.axis_index("prow")
    col = lax.axis_index("pcol")
    y, h, core = row // 4, (row // 2) % 2, row % 2
    z, w = col // 2, col % 2

    s = sigma_anc
    s_zm = move_z(s, 1)
    s_zp = move_z(s, -1)
    s_w = swap_w(s)
    l_h = swap_h(lower_blocks)
    pair = jnp.stack([lower_blocks, l_h])
    p_ym = move_y(pair, 1)
    p_yp = move_y(pair, -1)
    p_y2 = move_y(pair, 2)
    s_wzm = move_z(s_w, 1)
    s_wzp = move_z(s_w, -1)
    mine = (pair, p_ym, p_yp, p_y2)
    theirs = tuple(swap_core(x) for x in mine)
    half = s.shape[0] // 2
    up = move_z(jnp.stack([s_zm[:half], s_wzm[:half]]), 1)
    down = move_z(jnp.stack([s_zp[half:], s_wzp[half:]]), -1)

    my_rows = lax.dynamic_slice_in_dim(row_blocks, col * SUP, SUP, 0)
    order = jnp.arange(NA, dtype=jnp.int32)
    slots = jnp.sum(jnp.where(my_rows[:, :, None] == order, slot_of, 0), axis=2)
    sc = slots // 4
    dz = (sc // 2 - z) % 4
    group = jnp.where(dz == 0, 0, jnp.where(dz == 3, 1, jnp.where(dz == 1, 2, 3)))
    pos = (group * 2 + (sc % 2 + w) % 2) * 4 + slots % 4
    number = jnp.arange(1, NR + 1, dtype=jnp.int32)[None, :, None]
    inv = jnp.sum(jnp.where(pos[:, :, None] == order, number, 0), axis=1) - 1
    ours = row * 2 + jnp.arange(2, dtype=jnp.int32)
    own = jnp.sum(jnp.where(slots[:, :, None] == ours, number, 0), axis=1) - 1
    ys = jnp.stack([y, (y + 3) % 4, (y + 1) % 4, (y + 2) % 4])
    hs = jnp.stack([h, 1 - h])
    cs = jnp.stack([core, 1 - core])
    place = ((ys[None, :, None] * 2 + hs[None, None, :]) * 2 + cs[:, None, None]).reshape(-1) * 16
    place = place.astype(jnp.int32)

    hbm = pl.BlockSpec(memory_space=pl.ANY)
    smem = pl.BlockSpec(memory_space=pltpu.SMEM)
    vmem = pl.BlockSpec(memory_space=pltpu.VMEM)
    acc, blocks = pl.pallas_call(
        first_kernel,
        out_shape=(
            jax.ShapeDtypeStruct((SUP, 2 * B, B), jnp.float32),
            jax.ShapeDtypeStruct((SUP, NR, B, B), jnp.bfloat16),
        ),
        in_specs=[smem] * 2 + [hbm] * 14,
        out_specs=(hbm, hbm),
        scratch_shapes=[
            pltpu.VMEM((24, 2 * B, B), jnp.bfloat16),
            pltpu.VMEM((SUP, NR, B, B), jnp.bfloat16),
            pltpu.VMEM((SUP, 2 * B, B), jnp.float32),
            pltpu.SemaphoreType.DMA((24,)),
            pltpu.SemaphoreType.DMA((16,)),
            pltpu.SemaphoreType.DMA((2,)),
        ],
        compiler_params=pltpu.CompilerParams(vmem_limit_bytes=VMEM_LIMIT),
    )(inv, place, s, s_w, s_zm, s_wzm, s_zp, s_wzp, *mine, *theirs)

    sigma_off, keep, send = pl.pallas_call(
        last_kernel,
        out_shape=(
            jax.ShapeDtypeStruct((2 * B, SUP * B), jnp.bfloat16),
            jax.ShapeDtypeStruct((SUP, 8, 16, B), jnp.float32),
            jax.ShapeDtypeStruct((SUP, 8, 16, B), jnp.bfloat16),
        ),
        in_specs=[smem] * 3 + [hbm] * 4,
        out_specs=(vmem, vmem, vmem),
        scratch_shapes=[
            pltpu.VMEM((8, 2 * B, B), jnp.bfloat16),
            pltpu.VMEM((SUP, NR, B, B), jnp.bfloat16),
            pltpu.VMEM((SUP, 2 * B, B), jnp.float32),
            pltpu.VMEM((B, B), jnp.float32),
            pltpu.SemaphoreType.DMA((16,)),
            pltpu.SemaphoreType.DMA((2,)),
        ],
        compiler_params=pltpu.CompilerParams(vmem_limit_bytes=VMEM_LIMIT),
    )(inv, own, core.reshape(1).astype(jnp.int32), up, down, acc, blocks)

    one = keep + swap_core(send).astype(jnp.float32)
    one = one.reshape(SUP, 4, 2, 16, B)
    kept = lax.dynamic_index_in_dim(one, h, 2, keepdims=False)
    sent = lax.dynamic_index_in_dim(one, 1 - h, 2, keepdims=False).astype(jnp.bfloat16)
    two = kept + swap_h(sent).astype(jnp.float32)
    total = lax.dynamic_index_in_dim(two, y, 1, keepdims=False)
    narrow = two.astype(jnp.bfloat16)
    for step in (1, -1, 2):
        part = lax.dynamic_index_in_dim(narrow, (y + step) % 4, 1, keepdims=False)
        total = total + move_y(part, step).astype(jnp.float32)
    return sigma_off, inv_diag - total


def solution(mesh):
    in_specs = (P("prow", "pcol"), P("pcol", None, "prow", None), P(), P(), P("pcol", "prow", None))
    out_specs = (P("prow", "pcol"), P("pcol", "prow", None))
    return jax.shard_map(
        per_device, mesh=mesh, in_specs=in_specs, out_specs=out_specs, check_vma=False
    )
```

```python
import jax
import jax.numpy as jnp
from jax import lax
from jax.experimental import pallas as pl
from jax.experimental.pallas import tpu as pltpu
from jax.sharding import PartitionSpec as P

B = 256
NR = 16
SUP = 4
NA = 32
ROWS = 2 * B
VMEM_LIMIT = 4 * 1024 * 1024
FINAL_LIMIT = 16 * 1024 * 1024
AXES = ("prow", "pcol")


def permute(x, fn):
    pairs = []
    for y in range(4):
        for h in range(2):
            for co in range(2):
                for z in range(4):
                    for w in range(2):
                        ty, th, tc, tz, tw = fn(y, h, co, z, w)
                        target = ((ty % 4) * 4 + (th % 2) * 2 + tc % 2) * 8 + (tz % 4) * 2 + tw % 2
                        pairs.append(((y * 4 + h * 2 + co) * 8 + z * 2 + w, target))
    return lax.ppermute(x, AXES, pairs)


def z_first(x):
    return permute(x, lambda y, h, co, z, w: (y, h, co, z + 1 - 2 * co, w))


def z_second(x):
    return permute(x, lambda y, h, co, z, w: (y, h, co, z - 1 + 2 * co, w))


def y_first(x):
    return permute(x, lambda y, h, co, z, w: (y + 1 - 2 * co, h, co, z, w))


def y_second(x):
    return permute(x, lambda y, h, co, z, w: (y - 1 + 2 * co, h, co, z, w))


def move_y(x, step):
    return permute(x, lambda y, h, co, z, w: (y + step, h, co, z, w))


def swap_h(x):
    return permute(x, lambda y, h, co, z, w: (y, h + 1, co, z, w))


def swap_core(x):
    return permute(x, lambda y, h, co, z, w: (y, h, co + 1, z, w))


def swap_w(x):
    return permute(x, lambda y, h, co, z, w: (y, h, co, z, w + 1))


def tie(*arrays):
    return lax.optimization_barrier(arrays)


def in_hbm(*arrays):
    return [pltpu.with_memory_space_constraint(v, pltpu.HBM) for v in arrays]


def start_wait(copies):
    for copy in copies:
        copy.start()
    for copy in copies:
        copy.wait()


def slot_copies(parts, sv, sem):
    return [pltpu.make_async_copy(part, sv.at[n], sem.at[n]) for n, part in enumerate(parts)]


def columns(src, count):
    return [src.at[:, pl.ds(j * B, B)] for j in range(count)]


def hold_kernel(s, p1, p2, p3, sw, a1, a2, far, sv, sem):
    parts = []
    for src in (s, p1, p2, p3):
        parts += columns(src, 4)
    for src in (sw, a1, a2):
        parts += columns(src, 3)
    parts += [far.at[i] for i in range(4)]
    start_wait(slot_copies(parts, sv, sem))


def row_copies(parts, first, place_ref, lv, sem):
    copies = []
    for n, part in enumerate(parts):
        row = pl.multiple_of(place_ref[first + n], 16)
        copies.append(pltpu.make_async_copy(part, lv.at[:, :, pl.ds(row, 16), :], sem.at[n]))
    return copies


def panel_kernel(place_ref, x1, lh, r1, r2, t1, t2, lv, sem):
    parts = [x1.at[i] for i in range(4)] + [lh, r1, r2]
    parts += [t1.at[i] for i in range(4)] + [t2.at[i] for i in range(3)]
    start_wait(row_copies(parts, 0, place_ref, lv, sem))


def final_kernel(slot_ref, own_ref, place_ref, sv_in, lv_in, a3, r3, t3, off_out, send_out, sv, lv,
                 acc, s_sem, l_sem):
    loads = slot_copies(columns(a3, 3), sv.at[pl.ds(29, 3)], s_sem)
    loads += row_copies([r3, t3], 14, place_ref, lv, l_sem)
    start_wait(loads)
    for k in range(SUP):
        left = jnp.concatenate([sv[slot_ref[k, i]] for i in range(NR)], axis=1)
        acc[k] = jnp.dot(left, lv[k].reshape(NR * B, B), preferred_element_type=jnp.float32)
    for k in range(SUP):
        offs, owns = [], []
        for t in range(2):
            c = own_ref[k, t]
            alive = (c >= 0).astype(jnp.float32)
            off = (acc[k, pl.ds(t * B, B)] * -alive).astype(jnp.bfloat16)
            off_out[pl.ds(t * B, B), pl.ds(k * B, B)] = off
            offs.append(off)
            owns.append(lv[k, jnp.maximum(c, 0)])
        total = lax.dot_general(jnp.concatenate(owns, axis=0), jnp.concatenate(offs, axis=0),
                                (((0,), (0,)), ((), ())), preferred_element_type=jnp.float32)
        send_out[:, k] = (0.5 * (total + total.T)).astype(jnp.bfloat16).reshape(16, 16, B)


def per_device(sigma_anc, lower_blocks, row_blocks, slot_of, inv_diag):
    row = lax.axis_index("prow")
    col = lax.axis_index("pcol")
    y, h, core = row // 4, (row // 2) % 2, row % 2
    z, w = col // 2, col % 2

    my_rows = lax.dynamic_slice_in_dim(row_blocks, col * SUP, SUP, 0)
    order = jnp.arange(NA, dtype=jnp.int32)
    slots = jnp.sum(jnp.where(my_rows[:, :, None] == order, slot_of, 0), axis=2)
    sc = slots // 4
    dz = (sc // 2 - z) % 4
    one_away = jnp.where(dz == 3, 1 + core, 2 - core)
    group = jnp.where(dz == 0, 0, jnp.where(dz == 2, 3, one_away))
    near = group * 4 + slots % 4
    far = jnp.where(slots % 4 == 3, 25 + group, jnp.where(group == 3, 29, 16 + group * 3) + slots % 4)
    pos = jnp.where(sc % 2 == w, near, far).astype(jnp.int32)
    number = jnp.arange(1, NR + 1, dtype=jnp.int32)[None, :, None]
    ours = row * 2 + jnp.arange(2, dtype=jnp.int32)
    own = jnp.sum(jnp.where(slots[:, :, None] == ours, number, 0), axis=1) - 1
    rel = jnp.array([0, 3, 1, 2, 0, 3, 1, 0, 3, 1, 2, 0, 3, 1, 2, 2], jnp.int32)
    flip = jnp.array([0, 0, 0, 0, 1, 1, 1, 0, 0, 0, 0, 1, 1, 1, 1, 1], jnp.int32)
    cross = jnp.array([0, 0, 0, 0, 0, 0, 0, 1, 1, 1, 1, 1, 1, 1, 0, 1], jnp.int32)
    cs = (core + cross) % 2
    place = ((((y + rel * (1 + 2 * cs)) % 4) * 2 + (h + flip) % 2) * 2 + cs) * 16
    place = place.astype(jnp.int32)

    s, l = sigma_anc, lower_blocks
    p1 = z_first(s)
    p2 = z_second(s)
    sw = swap_w(s[:, :3 * B])
    lh = swap_h(l)
    q1 = y_first(l)
    q2 = y_second(l)
    q3 = y_first(q1)
    p3 = z_first(p1)
    p2, sw, lh, q1, q2, q3 = tie(p2, sw, lh, q1, q2, q3)
    r1 = y_first(lh)
    r2 = y_second(lh)
    x1 = jnp.stack([l, q1, q2, q3])
    t1 = swap_core(x1)
    sw, p3 = tie(sw, p3)
    a1 = z_first(sw)
    a2 = z_second(sw)
    far = swap_w(jnp.stack([v[:, 3 * B:] for v in (s, p1, p2, p3)]))
    r3 = y_first(r1)
    t2 = swap_core(jnp.stack([lh, r1, r2]))
    a1, a2, far, r3 = tie(a1, a2, far, r3)
    a3 = z_first(a1)
    t3 = swap_core(r3)
    s, p1, p2, p3, sw, a1, a2, a3, far = in_hbm(s, p1, p2, p3, sw, a1, a2, a3, far)
    lh, r1, r2, r3, x1, t1, t2, t3 = in_hbm(lh, r1, r2, r3, x1, t1, t2, t3)

    hbm = pl.BlockSpec(memory_space=pltpu.HBM)
    smem = pl.BlockSpec(memory_space=pltpu.SMEM)
    vmem = pl.BlockSpec(memory_space=pltpu.VMEM)
    params = pltpu.CompilerParams(vmem_limit_bytes=VMEM_LIMIT)
    final_params = pltpu.CompilerParams(vmem_limit_bytes=FINAL_LIMIT)
    panel_shape = pltpu.VMEM((SUP, NR, B, B), jnp.bfloat16)
    held_shape = pltpu.VMEM((NA, ROWS, B), jnp.bfloat16)
    held = pl.pallas_call(
        hold_kernel,
        out_shape=held_shape,
        in_specs=[hbm] * 8,
        out_specs=vmem,
        scratch_shapes=[pltpu.SemaphoreType.DMA((29,))],
        compiler_params=params,
    )(s, p1, p2, p3, sw, a1, a2, far)
    held = pltpu.with_memory_space_constraint(held, pltpu.VMEM)
    blocks = pl.pallas_call(
        panel_kernel,
        out_shape=panel_shape,
        in_specs=[smem] + [hbm] * 6,
        out_specs=vmem,
        scratch_shapes=[pltpu.SemaphoreType.DMA((14,))],
        compiler_params=params,
    )(place, x1, lh, r1, r2, t1, t2)
    blocks = pltpu.with_memory_space_constraint(blocks, pltpu.VMEM)
    sigma_off, send, _, _ = pl.pallas_call(
        final_kernel,
        out_shape=(
            jax.ShapeDtypeStruct((ROWS, SUP * B), jnp.bfloat16),
            jax.ShapeDtypeStruct((16, SUP, 16, B), jnp.bfloat16),
            held_shape,
            panel_shape,
        ),
        in_specs=[smem] * 3 + [vmem] * 2 + [hbm] * 3,
        out_specs=(vmem, vmem, vmem, vmem),
        input_output_aliases={3: 2, 4: 3},
        scratch_shapes=[
            pltpu.VMEM((SUP, ROWS, B), jnp.float32),
            pltpu.SemaphoreType.DMA((3,)),
            pltpu.SemaphoreType.DMA((2,)),
        ],
        compiler_params=final_params,
    )(pos, own, place, held, blocks, a3, r3, t3)

    parts = lax.all_to_all(send, "prow", split_axis=0, concat_axis=0, tiled=True)
    total = jnp.sum(parts.astype(jnp.float32), axis=0)
    return sigma_off, inv_diag - total


def solution(mesh):
    in_specs = (P("prow", "pcol"), P("pcol", None, "prow", None), P(), P(), P("pcol", "prow", None))
    out_specs = (P("prow", "pcol"), P("pcol", "prow", None))
    return jax.shard_map(
        per_device, mesh=mesh, in_specs=in_specs, out_specs=out_specs, check_vma=False
    )
```

```python
import jax
import jax.numpy as jnp
from jax import lax
from jax.experimental import pallas as pl
from jax.experimental.pallas import tpu as pltpu
from jax.sharding import PartitionSpec as P

B = 256
NR = 16
SUP = 4
NA = 32
ROWS = 2 * B
VMEM_LIMIT = 4 * 1024 * 1024
FINAL_LIMIT = 16 * 1024 * 1024
AXES = ("prow", "pcol")


def permute(x, fn):
    pairs = []
    for y in range(4):
        for h in range(2):
            for co in range(2):
                for z in range(4):
                    for w in range(2):
                        ty, th, tc, tz, tw = fn(y, h, co, z, w)
                        target = ((ty % 4) * 4 + (th % 2) * 2 + tc % 2) * 8 + (tz % 4) * 2 + tw % 2
                        pairs.append(((y * 4 + h * 2 + co) * 8 + z * 2 + w, target))
    return lax.ppermute(x, AXES, pairs)


def z_first(x):
    return permute(x, lambda y, h, co, z, w: (y, h, co, z + 1 - 2 * co, w))


def z_second(x):
    return permute(x, lambda y, h, co, z, w: (y, h, co, z - 1 + 2 * co, w))


def y_first(x):
    return permute(x, lambda y, h, co, z, w: (y + 1 - 2 * co, h, co, z, w))


def y_second(x):
    return permute(x, lambda y, h, co, z, w: (y - 1 + 2 * co, h, co, z, w))


def move_y(x, step):
    return permute(x, lambda y, h, co, z, w: (y + step, h, co, z, w))


def swap_h(x):
    return permute(x, lambda y, h, co, z, w: (y, h + 1, co, z, w))


def swap_core(x):
    return permute(x, lambda y, h, co, z, w: (y, h, co + 1, z, w))


def swap_w(x):
    return permute(x, lambda y, h, co, z, w: (y, h, co, z, w + 1))


def tie(*arrays):
    return lax.optimization_barrier(arrays)


def in_hbm(*arrays):
    return [pltpu.with_memory_space_constraint(v, pltpu.HBM) for v in arrays]


def start_wait(copies):
    for copy in copies:
        copy.start()
    for copy in copies:
        copy.wait()


def slot_copies(parts, sv, sem):
    return [pltpu.make_async_copy(part, sv.at[n], sem.at[n]) for n, part in enumerate(parts)]


def columns(src, count):
    return [src.at[:, pl.ds(j * B, B)] for j in range(count)]


def hold_kernel(s, p1, p2, p3, sw, a1, a2, far, sv, sem):
    parts = []
    for src in (s, p1, p2, p3, sw):
        parts += columns(src, 4)
    for i, src in enumerate((a1, a2)):
        parts += columns(src, 3) + [far.at[i]]
    parts.append(far.at[2])
    start_wait(slot_copies(parts, sv, sem))


def row_copies(parts, first, place_ref, lv, sem):
    copies = []
    for n, part in enumerate(parts):
        row = pl.multiple_of(place_ref[first + n], 16)
        copies.append(pltpu.make_async_copy(part, lv.at[:, :, pl.ds(row, 16), :], sem.at[n]))
    return copies


def panel_kernel(place_ref, x0, x1, lh, r1, r2, tx0, tx1, t0, t2, lv, sem):
    parts = [x0.at[0], x0.at[1], x1.at[0], x1.at[1], lh, r1, r2]
    parts += [tx0.at[0], tx0.at[1], tx1.at[0], tx1.at[1], t0, t2.at[0], t2.at[1]]
    start_wait(row_copies(parts, 0, place_ref, lv, sem))


def final_kernel(slot_ref, own_ref, place_ref, core_ref, sv_in, lv_in, a3, r3, t3, off_out, keep_out, send_out, sv, lv,
                 acc, s_sem, l_sem):
    loads = slot_copies(columns(a3, 3), sv.at[pl.ds(29, 3)], s_sem)
    loads += row_copies([r3, t3], 14, place_ref, lv, l_sem)
    start_wait(loads)
    for k in range(SUP):
        left = jnp.concatenate([sv[slot_ref[k, i]] for i in range(NR)], axis=1)
        acc[k] = jnp.dot(left, lv[k].reshape(NR * B, B), preferred_element_type=jnp.float32)
    core = core_ref[0]
    for k in range(SUP):
        offs, owns = [], []
        for t in range(2):
            c = own_ref[k, t]
            alive = (c >= 0).astype(jnp.float32)
            off = (acc[k, pl.ds(t * B, B)] * -alive).astype(jnp.bfloat16)
            off_out[pl.ds(t * B, B), pl.ds(k * B, B)] = off
            offs.append(off)
            owns.append(lv[k, jnp.maximum(c, 0)])
        total = lax.dot_general(jnp.concatenate(owns, axis=0), jnp.concatenate(offs, axis=0),
                                (((0,), (0,)), ((), ())), preferred_element_type=jnp.float32)
        part = (0.5 * (total + total.T)).reshape(8, 2, 16, B)
        keep_out[:, k] = jnp.where(core == 0, part[:, 0], part[:, 1])
        send_out[:, k] = jnp.where(core == 0, part[:, 1], part[:, 0]).astype(jnp.bfloat16)


def per_device(sigma_anc, lower_blocks, row_blocks, slot_of, inv_diag):
    row = lax.axis_index("prow")
    col = lax.axis_index("pcol")
    y, h, core = row // 4, (row // 2) % 2, row % 2
    z, w = col // 2, col % 2

    my_rows = lax.dynamic_slice_in_dim(row_blocks, col * SUP, SUP, 0)
    order = jnp.arange(NA, dtype=jnp.int32)
    slots = jnp.sum(jnp.where(my_rows[:, :, None] == order, slot_of, 0), axis=2)
    sc = slots // 4
    dz = (sc // 2 - z) % 4
    one_away = jnp.where(dz == 3, 1 + core, 2 - core)
    group = jnp.where(dz == 0, 0, jnp.where(dz == 2, 3, one_away))
    near = group * 4 + slots % 4
    far = jnp.where(group == 3, jnp.where(slots % 4 == 3, 28, 29 + slots % 4), 16 + group * 4 + slots % 4)
    pos = jnp.where(sc % 2 == w, near, far).astype(jnp.int32)
    number = jnp.arange(1, NR + 1, dtype=jnp.int32)[None, :, None]
    ours = row * 2 + jnp.arange(2, dtype=jnp.int32)
    own = jnp.sum(jnp.where(slots[:, :, None] == ours, number, 0), axis=1) - 1
    rel = jnp.array([0, 3, 1, 2, 0, 3, 1, 0, 3, 1, 2, 0, 3, 1, 2, 2], jnp.int32)
    flip = jnp.array([0, 0, 0, 0, 1, 1, 1, 0, 0, 0, 0, 1, 1, 1, 1, 1], jnp.int32)
    cross = jnp.array([0, 0, 0, 0, 0, 0, 0, 1, 1, 1, 1, 1, 1, 1, 0, 1], jnp.int32)
    cs = (core + cross) % 2
    place = ((((y + rel * (1 + 2 * cs)) % 4) * 2 + (h + flip) % 2) * 2 + cs) * 16
    place = place.astype(jnp.int32)

    s, l = sigma_anc, lower_blocks
    p1 = z_first(s)
    p2 = z_second(s)
    sw = swap_w(s)
    wa = sw[:, :3 * B]
    q1 = y_first(l)
    q2 = y_second(l)
    p1, q1, q2 = tie(p1, q1, q2)
    p3 = z_first(p1)
    lh = swap_h(l)
    q3 = y_first(q1)
    p2, p3, wa, lh, q3 = tie(p2, p3, wa, lh, q3)
    a1 = z_first(wa)
    a2 = z_second(wa)
    far = swap_w(jnp.stack([v[:, 3 * B:] for v in (p1, p2, p3)]))
    r1 = y_first(lh)
    r2 = y_second(lh)
    r1, r2, q1, q3 = tie(r1, r2, q1, q3)
    r3 = y_first(r1)
    x0 = jnp.stack([l, q1])
    x1 = jnp.stack([q2, q3])
    tx0 = swap_core(x0)
    tx1 = swap_core(x1)
    t0 = swap_core(lh)
    t2 = swap_core(jnp.stack([r1, r2]))
    a1, a2, far = tie(a1, a2, far)
    a3 = z_first(a1)
    t3 = swap_core(r3)
    s, p1, p2, p3, sw, a1, a2, a3, far = in_hbm(s, p1, p2, p3, sw, a1, a2, a3, far)
    lh, r1, r2, r3, x0, x1 = in_hbm(lh, r1, r2, r3, x0, x1)
    t0, tx0, tx1, t2, t3 = in_hbm(t0, tx0, tx1, t2, t3)

    hbm = pl.BlockSpec(memory_space=pltpu.HBM)
    smem = pl.BlockSpec(memory_space=pltpu.SMEM)
    vmem = pl.BlockSpec(memory_space=pltpu.VMEM)
    params = pltpu.CompilerParams(vmem_limit_bytes=VMEM_LIMIT)
    final_params = pltpu.CompilerParams(vmem_limit_bytes=FINAL_LIMIT)
    panel_shape = pltpu.VMEM((SUP, NR, B, B), jnp.bfloat16)
    held_shape = pltpu.VMEM((NA, ROWS, B), jnp.bfloat16)
    held = pl.pallas_call(
        hold_kernel,
        out_shape=held_shape,
        in_specs=[hbm] * 8,
        out_specs=vmem,
        scratch_shapes=[pltpu.SemaphoreType.DMA((29,))],
        compiler_params=params,
    )(s, p1, p2, p3, sw, a1, a2, far)
    held = pltpu.with_memory_space_constraint(held, pltpu.VMEM)
    blocks = pl.pallas_call(
        panel_kernel,
        out_shape=panel_shape,
        in_specs=[smem] + [hbm] * 9,
        out_specs=vmem,
        scratch_shapes=[pltpu.SemaphoreType.DMA((14,))],
        compiler_params=params,
    )(place, x0, x1, lh, r1, r2, tx0, tx1, t0, t2)
    blocks = pltpu.with_memory_space_constraint(blocks, pltpu.VMEM)
    sigma_off, keep, send, _, _ = pl.pallas_call(
        final_kernel,
        out_shape=(
            jax.ShapeDtypeStruct((ROWS, SUP * B), jnp.bfloat16),
            jax.ShapeDtypeStruct((8, SUP, 16, B), jnp.float32),
            jax.ShapeDtypeStruct((8, SUP, 16, B), jnp.bfloat16),
            held_shape,
            panel_shape,
        ),
        in_specs=[smem] * 4 + [vmem] * 2 + [hbm] * 3,
        out_specs=(vmem,) * 5,
        input_output_aliases={4: 3, 5: 4},
        scratch_shapes=[
            pltpu.VMEM((SUP, ROWS, B), jnp.float32),
            pltpu.SemaphoreType.DMA((3,)),
            pltpu.SemaphoreType.DMA((2,)),
        ],
        compiler_params=final_params,
    )(pos, own, place, core.reshape(1).astype(jnp.int32), held, blocks, a3, r3, t3)

    halves = (keep + swap_core(send).astype(jnp.float32)).astype(jnp.bfloat16)
    parts = lax.all_to_all(halves, "prow", split_axis=0, concat_axis=0, tiled=True,
                           axis_index_groups=[list(range(c, 16, 2)) for c in range(2)])
    total = jnp.sum(parts.astype(jnp.float32), axis=0)
    return sigma_off, inv_diag - total


def solution(mesh):
    in_specs = (P("prow", "pcol"), P("pcol", None, "prow", None), P(), P(), P("pcol", "prow", None))
    out_specs = (P("prow", "pcol"), P("pcol", "prow", None))
    return jax.shard_map(
        per_device, mesh=mesh, in_specs=in_specs, out_specs=out_specs, check_vma=False
    )
```

```python
import jax
import jax.numpy as jnp
from jax import lax
from jax.experimental import pallas as pl
from jax.experimental.pallas import tpu as pltpu
from jax.sharding import PartitionSpec as P

B = 256
NR = 16
SUP = 4
NA = 32
EARLY = 13
ROWS = 2 * B
VMEM_LIMIT = 16 * 1024 * 1024
AXES = ("prow", "pcol")


def permute(x, fn):
    pairs = []
    for y in range(4):
        for h in range(2):
            for co in range(2):
                for z in range(4):
                    for w in range(2):
                        ty, th, tc, tz, tw = fn(y, h, co, z, w)
                        target = ((ty % 4) * 4 + (th % 2) * 2 + tc % 2) * 8 + (tz % 4) * 2 + tw % 2
                        pairs.append(((y * 4 + h * 2 + co) * 8 + z * 2 + w, target))
    return lax.ppermute(x, AXES, pairs)


def z_first(x):
    return permute(x, lambda y, h, co, z, w: (y, h, co, z + 1 - 2 * co, w))


def z_second(x):
    return permute(x, lambda y, h, co, z, w: (y, h, co, z - 1 + 2 * co, w))


def y_first(x):
    return permute(x, lambda y, h, co, z, w: (y + 1 - 2 * co, h, co, z, w))


def y_second(x):
    return permute(x, lambda y, h, co, z, w: (y - 1 + 2 * co, h, co, z, w))


def move_y(x, step):
    return permute(x, lambda y, h, co, z, w: (y + step, h, co, z, w))


def swap_h(x):
    return permute(x, lambda y, h, co, z, w: (y, h + 1, co, z, w))


def swap_core(x):
    return permute(x, lambda y, h, co, z, w: (y, h, co + 1, z, w))


def swap_w(x):
    return permute(x, lambda y, h, co, z, w: (y, h, co, z, w + 1))


def tie(*arrays):
    return lax.optimization_barrier(arrays)


def in_hbm(*arrays):
    return [pltpu.with_memory_space_constraint(v, pltpu.HBM) for v in arrays]


def start_wait(copies):
    for copy in copies:
        copy.start()
    for copy in copies:
        copy.wait()


def slot_copies(parts, sv, sem):
    return [pltpu.make_async_copy(part, sv.at[n], sem.at[n]) for n, part in enumerate(parts)]


def columns(src, count):
    return [src.at[:, pl.ds(j * B, B)] for j in range(count)]


def hold_kernel(s, p1, p2, p3, sw, a1, a2, far, sv, sem):
    parts = []
    for src in (s, p1, p2, p3, sw):
        parts += columns(src, 4)
    for i, src in enumerate((a1, a2)):
        parts += columns(src, 3) + [far.at[i]]
    start_wait(slot_copies(parts + [far.at[2]], sv, sem))


def row_copies(parts, first, place_ref, lv, sem):
    copies = []
    for n, part in enumerate(parts):
        row = pl.multiple_of(place_ref[first + n], 16)
        copies.append(pltpu.make_async_copy(part, lv.at[:, :, pl.ds(row, 16), :], sem.at[n]))
    return copies


def panel_kernel(place_ref, x0, x1, lh, r1, r2, tx0, tx1, t0, t2, lv, sem):
    parts = [x0.at[0], x0.at[1], x1.at[0], x1.at[1], lh, r1, r2]
    parts += [tx0.at[0], tx0.at[1], tx1.at[0], tx1.at[1], t0, t2.at[0], t2.at[1]]
    start_wait(row_copies(parts, 0, place_ref, lv, sem))


def product(slot_ref, block_ref, k, first, count, sv, lv):
    left = jnp.concatenate([sv[slot_ref[k, i]] for i in range(first, first + count)], axis=1)
    right = jnp.concatenate([lv[k, block_ref[k, i]] for i in range(first, first + count)], axis=0)
    return jnp.dot(left, right, preferred_element_type=jnp.float32)


def main_kernel(slot_ref, block_ref, place_ref, sv, lv_in, r3, t3, lv, acc, sem):
    start_wait(row_copies([r3, t3], 14, place_ref, lv, sem))
    for k in range(SUP):
        acc[k] = product(slot_ref, block_ref, k, 0, EARLY, sv, lv)


def late_kernel(slot_ref, block_ref, own_ref, core_ref, sv_in, lv, acc_in, a3, off_out, keep_out, send_out, sv,
                acc, off_ref, sem):
    for j in range(3):
        sv[29 + j] = a3[:, j * B:(j + 1) * B]
    stores = []
    core = core_ref[0]
    for k in range(SUP):
        acc[k] = acc_in[k] + product(slot_ref, block_ref, k, EARLY, NR - EARLY, sv, lv)
    for k in range(SUP):
        offs, owns = [], []
        for t in range(2):
            c = own_ref[k, t]
            alive = (c >= 0).astype(jnp.float32)
            off = (acc[k, pl.ds(t * B, B)] * -alive).astype(jnp.bfloat16)
            off_ref[k, pl.ds(t * B, B)] = off
            offs.append(off)
            owns.append(lv[k, jnp.maximum(c, 0)])
        stores.append(pltpu.make_async_copy(off_ref.at[k], off_out.at[:, pl.ds(k * B, B)], sem.at[k]))
        stores[-1].start()
        total = lax.dot_general(jnp.concatenate(owns, axis=0), jnp.concatenate(offs, axis=0),
                                (((0,), (0,)), ((), ())), preferred_element_type=jnp.float32)
        part = (0.5 * (total + total.T)).reshape(8, 2, 16, B)
        keep_out[:, k] = jnp.where(core == 0, part[:, 0], part[:, 1])
        send_out[:, k] = jnp.where(core == 0, part[:, 1], part[:, 0]).astype(jnp.bfloat16)
    for store in stores:
        store.wait()


def per_device(sigma_anc, lower_blocks, row_blocks, slot_of, inv_diag):
    row = lax.axis_index("prow")
    col = lax.axis_index("pcol")
    y, h, core = row // 4, (row // 2) % 2, row % 2
    z, w = col // 2, col % 2

    my_rows = lax.dynamic_slice_in_dim(row_blocks, col * SUP, SUP, 0)
    order = jnp.arange(NA, dtype=jnp.int32)
    slots = jnp.sum(jnp.where(my_rows[:, :, None] == order, slot_of, 0), axis=2)
    sc = slots // 4
    dz = (sc // 2 - z) % 4
    one_away = jnp.where(dz == 3, 1 + core, 2 - core)
    group = jnp.where(dz == 0, 0, jnp.where(dz == 2, 3, one_away))
    near = group * 4 + slots % 4
    far = jnp.where(group == 3, jnp.where(slots % 4 == 3, 28, 29 + slots % 4), 16 + group * 4 + slots % 4)
    pos = jnp.where(sc % 2 == w, near, far).astype(jnp.int32)
    rank = jnp.sum((pos[:, None, :] < pos[:, :, None]).astype(jnp.int32), axis=2)
    ranked = rank[:, :, None] == jnp.arange(NR, dtype=jnp.int32)
    index = jnp.arange(NR, dtype=jnp.int32)[None, :, None]
    sorted_slots = jnp.sum(jnp.where(ranked, pos[:, :, None], 0), axis=1)
    sorted_blocks = jnp.sum(jnp.where(ranked, index, 0), axis=1)
    number = jnp.arange(1, NR + 1, dtype=jnp.int32)[None, :, None]
    ours = row * 2 + jnp.arange(2, dtype=jnp.int32)
    own = jnp.sum(jnp.where(slots[:, :, None] == ours, number, 0), axis=1) - 1
    rel = jnp.array([0, 3, 1, 2, 0, 3, 1, 0, 3, 1, 2, 0, 3, 1, 2, 2], jnp.int32)
    flip = jnp.array([0, 0, 0, 0, 1, 1, 1, 0, 0, 0, 0, 1, 1, 1, 1, 1], jnp.int32)
    cross = jnp.array([0, 0, 0, 0, 0, 0, 0, 1, 1, 1, 1, 1, 1, 1, 0, 1], jnp.int32)
    cs = (core + cross) % 2
    place = ((((y + rel * (1 + 2 * cs)) % 4) * 2 + (h + flip) % 2) * 2 + cs) * 16
    place = place.astype(jnp.int32)

    s, l = sigma_anc, lower_blocks
    p1 = z_first(s)
    p2 = z_second(s)
    sw = swap_w(s)
    wa = sw[:, :3 * B]
    q1 = y_first(l)
    q2 = y_second(l)
    p1, q1, q2 = tie(p1, q1, q2)
    p3 = z_first(p1)
    lh = swap_h(l)
    q3 = y_first(q1)
    p2, p3, wa, lh, q3 = tie(p2, p3, wa, lh, q3)
    a1 = z_first(wa)
    a2 = z_second(wa)
    far = swap_w(jnp.stack([v[:, 3 * B:] for v in (p1, p2, p3)]))
    r1 = y_first(lh)
    r2 = y_second(lh)
    r1, r2, q1, q3 = tie(r1, r2, q1, q3)
    r3 = y_first(r1)
    x0 = jnp.stack([l, q1])
    x1 = jnp.stack([q2, q3])
    tx0 = swap_core(x0)
    tx1 = swap_core(x1)
    t0 = swap_core(lh)
    t2 = swap_core(jnp.stack([r1, r2]))
    a1, a2, far = tie(a1, a2, far)
    a3 = z_first(a1)
    t3 = swap_core(r3)
    s, p1, p2, p3, sw, a1, a2, far = in_hbm(s, p1, p2, p3, sw, a1, a2, far)
    a3 = pltpu.with_memory_space_constraint(a3, pltpu.VMEM)
    lh, r1, r2, x0, x1 = in_hbm(lh, r1, r2, x0, x1)
    t0, tx0, tx1, t2 = in_hbm(t0, tx0, tx1, t2)
    r3, t3 = [pltpu.with_memory_space_constraint(v, pltpu.VMEM) for v in (r3, t3)]

    hbm = pl.BlockSpec(memory_space=pltpu.HBM)
    smem = pl.BlockSpec(memory_space=pltpu.SMEM)
    vmem = pl.BlockSpec(memory_space=pltpu.VMEM)
    params = pltpu.CompilerParams(vmem_limit_bytes=VMEM_LIMIT)
    panel_shape = pltpu.VMEM((SUP, NR, B, B), jnp.bfloat16)
    held_shape = pltpu.VMEM((NA, ROWS, B), jnp.bfloat16)
    acc_shape = pltpu.VMEM((SUP, ROWS, B), jnp.float32)
    held = pl.pallas_call(
        hold_kernel,
        out_shape=held_shape,
        in_specs=[hbm] * 8,
        out_specs=vmem,
        scratch_shapes=[pltpu.SemaphoreType.DMA((29,))],
        compiler_params=params,
    )(s, p1, p2, p3, sw, a1, a2, far)
    blocks = pl.pallas_call(
        panel_kernel,
        out_shape=panel_shape,
        in_specs=[smem] + [hbm] * 9,
        out_specs=vmem,
        scratch_shapes=[pltpu.SemaphoreType.DMA((14,))],
        compiler_params=params,
    )(place, x0, x1, lh, r1, r2, tx0, tx1, t0, t2)
    held, blocks = [pltpu.with_memory_space_constraint(v, pltpu.VMEM) for v in (held, blocks)]
    blocks, acc = pl.pallas_call(
        main_kernel,
        out_shape=(panel_shape, acc_shape),
        in_specs=[smem] * 3 + [vmem] * 4,
        out_specs=(vmem, vmem),
        input_output_aliases={4: 0},
        scratch_shapes=[pltpu.SemaphoreType.DMA((2,))],
        compiler_params=params,
    )(sorted_slots, sorted_blocks, place, held, blocks, r3, t3)
    blocks, acc = [pltpu.with_memory_space_constraint(v, pltpu.VMEM) for v in (blocks, acc)]
    sigma_off, keep, send, _ = pl.pallas_call(
        late_kernel,
        out_shape=(
            jax.ShapeDtypeStruct((ROWS, SUP * B), jnp.bfloat16),
            jax.ShapeDtypeStruct((8, SUP, 16, B), jnp.float32),
            jax.ShapeDtypeStruct((8, SUP, 16, B), jnp.bfloat16),
            held_shape,
        ),
        in_specs=[smem] * 4 + [vmem] * 4,
        out_specs=(hbm,) + (vmem,) * 3,
        input_output_aliases={4: 3},
        scratch_shapes=[
            pltpu.VMEM((SUP, ROWS, B), jnp.float32),
            pltpu.VMEM((SUP, ROWS, B), jnp.bfloat16),
            pltpu.SemaphoreType.DMA((SUP,)),
        ],
        compiler_params=params,
    )(sorted_slots, sorted_blocks, own, core.reshape(1).astype(jnp.int32), held, blocks, acc, a3)

    halves = (keep + swap_core(send).astype(jnp.float32)).astype(jnp.bfloat16)
    parts = lax.all_to_all(halves, "prow", split_axis=0, concat_axis=0, tiled=True,
                           axis_index_groups=[list(range(c, 16, 2)) for c in range(2)])
    total = jnp.sum(parts.astype(jnp.float32), axis=0)
    return sigma_off, inv_diag - total


def solution(mesh):
    in_specs = (P("prow", "pcol"), P("pcol", None, "prow", None), P(), P(), P("pcol", "prow", None))
    out_specs = (P("prow", "pcol"), P("pcol", "prow", None))
    return jax.shard_map(
        per_device, mesh=mesh, in_specs=in_specs, out_specs=out_specs, check_vma=False
    )
```

```python
import jax
import jax.numpy as jnp
from jax import lax
from jax.experimental import pallas as pl
from jax.experimental.pallas import tpu as pltpu
from jax.sharding import PartitionSpec as P

B = 256
NR = 16
SUP = 4
NA = 32
EARLY = 13
ROWS = 2 * B
VMEM_LIMIT = 16 * 1024 * 1024
AXES = ("prow", "pcol")


def permute(x, fn):
    pairs = []
    for y in range(4):
        for h in range(2):
            for co in range(2):
                for z in range(4):
                    for w in range(2):
                        ty, th, tc, tz, tw = fn(y, h, co, z, w)
                        target = ((ty % 4) * 4 + (th % 2) * 2 + tc % 2) * 8 + (tz % 4) * 2 + tw % 2
                        pairs.append(((y * 4 + h * 2 + co) * 8 + z * 2 + w, target))
    return lax.ppermute(x, AXES, pairs)


def z_first(x):
    return permute(x, lambda y, h, co, z, w: (y, h, co, z + 1 - 2 * co, w))


def z_second(x):
    return permute(x, lambda y, h, co, z, w: (y, h, co, z - 1 + 2 * co, w))


def y_first(x):
    return permute(x, lambda y, h, co, z, w: (y + 1 - 2 * co, h, co, z, w))


def y_second(x):
    return permute(x, lambda y, h, co, z, w: (y - 1 + 2 * co, h, co, z, w))


def move_y(x, step):
    return permute(x, lambda y, h, co, z, w: (y + step, h, co, z, w))


def swap_h(x):
    return permute(x, lambda y, h, co, z, w: (y, h + 1, co, z, w))


def swap_core(x):
    return permute(x, lambda y, h, co, z, w: (y, h, co + 1, z, w))


def swap_w(x):
    return permute(x, lambda y, h, co, z, w: (y, h, co, z, w + 1))


def tie(*arrays):
    return lax.optimization_barrier(arrays)


def in_hbm(*arrays):
    return [pltpu.with_memory_space_constraint(v, pltpu.HBM) for v in arrays]


def start_wait(copies):
    for copy in copies:
        copy.start()
    for copy in copies:
        copy.wait()


def slot_copies(parts, sv, sem):
    return [pltpu.make_async_copy(part, sv.at[n], sem.at[n]) for n, part in enumerate(parts)]


def columns(src, count):
    return [src.at[:, pl.ds(j * B, B)] for j in range(count)]


def hold_kernel(s, p1, p2, p3, sw, a1, a2, far, sv, sem):
    parts = []
    for src in (s, p1, p2, p3, sw):
        parts += columns(src, 4)
    for i, src in enumerate((a1, a2)):
        parts += columns(src, 3) + [far.at[i]]
    start_wait(slot_copies(parts + [far.at[2]], sv, sem))


def row_copies(parts, first, place_ref, lv, sem):
    copies = []
    for n, part in enumerate(parts):
        row = pl.multiple_of(place_ref[first + n], 16)
        copies.append(pltpu.make_async_copy(part, lv.at[:, :, pl.ds(row, 16), :], sem.at[n]))
    return copies


def panel_kernel(place_ref, x0, x1, lh, r1, r2, tx0, tx1, t0, t2, lv, sem):
    parts = [x0.at[0], x0.at[1], x1.at[0], x1.at[1], lh, r1, r2]
    parts += [tx0.at[0], tx0.at[1], tx1.at[0], tx1.at[1], t0, t2.at[0], t2.at[1]]
    start_wait(row_copies(parts, 0, place_ref, lv, sem))


def product(slot_ref, block_ref, k, first, count, sv, lv):
    left = jnp.concatenate([sv[slot_ref[k, i]] for i in range(first, first + count)], axis=1)
    right = jnp.concatenate([lv[k, block_ref[k, i]] for i in range(first, first + count)], axis=0)
    return jnp.dot(left, right, preferred_element_type=jnp.float32)


def main_kernel(slot_ref, block_ref, place_ref, sv, lv_in, r3, t3, lv, acc, sem):
    start_wait(row_copies([r3, t3], 14, place_ref, lv, sem))
    for k in range(SUP):
        acc[k] = product(slot_ref, block_ref, k, 0, EARLY, sv, lv)


def late_kernel(slot_ref, block_ref, own_ref, core_ref, sv_in, lv, acc_in, a3, off_out, keep_out, send_out, sv,
                acc, off_ref, sem):
    for j in range(3):
        sv[29 + j] = a3[:, j * B:(j + 1) * B]
    stores = []
    core = core_ref[0]
    for k in range(SUP):
        acc[k] = acc_in[k] + product(slot_ref, block_ref, k, EARLY, NR - EARLY, sv, lv)
    for k in range(SUP):
        offs, owns = [], []
        for t in range(2):
            c = own_ref[k, t]
            alive = (c >= 0).astype(jnp.float32)
            off = (acc[k, pl.ds(t * B, B)] * -alive).astype(jnp.bfloat16)
            off_ref[k, pl.ds(t * B, B)] = off
            offs.append(off)
            owns.append(lv[k, jnp.maximum(c, 0)])
        stores.append(pltpu.make_async_copy(off_ref.at[k], off_out.at[:, pl.ds(k * B, B)], sem.at[k]))
        stores[-1].start()
        total = lax.dot_general(jnp.concatenate(owns, axis=0), jnp.concatenate(offs, axis=0),
                                (((0,), (0,)), ((), ())), preferred_element_type=jnp.float32)
        part = (0.5 * (total + total.T)).reshape(8, 2, 16, B)
        keep_out[:, k] = jnp.where(core == 0, part[:, 0], part[:, 1])
        send_out[:, k] = jnp.where(core == 0, part[:, 1], part[:, 0]).astype(jnp.bfloat16)
    for store in stores:
        store.wait()


def per_device(sigma_anc, lower_blocks, row_blocks, slot_of, inv_diag):
    row = lax.axis_index("prow")
    col = lax.axis_index("pcol")
    y, h, core = row // 4, (row // 2) % 2, row % 2
    z, w = col // 2, col % 2

    my_rows = lax.dynamic_slice_in_dim(row_blocks, col * SUP, SUP, 0)
    order = jnp.arange(NA, dtype=jnp.int32)
    slots = jnp.sum(jnp.where(my_rows[:, :, None] == order, slot_of, 0), axis=2)
    sc = slots // 4
    dz = (sc // 2 - z) % 4
    one_away = jnp.where(dz == 3, 1 + core, 2 - core)
    group = jnp.where(dz == 0, 0, jnp.where(dz == 2, 3, one_away))
    near = group * 4 + slots % 4
    far = jnp.where(group == 3, jnp.where(slots % 4 == 3, 28, 29 + slots % 4), 16 + group * 4 + slots % 4)
    pos = jnp.where(sc % 2 == w, near, far).astype(jnp.int32)
    rank = jnp.sum((pos[:, None, :] < pos[:, :, None]).astype(jnp.int32), axis=2)
    ranked = rank[:, :, None] == jnp.arange(NR, dtype=jnp.int32)
    index = jnp.arange(NR, dtype=jnp.int32)[None, :, None]
    sorted_slots = jnp.sum(jnp.where(ranked, pos[:, :, None], 0), axis=1)
    sorted_blocks = jnp.sum(jnp.where(ranked, index, 0), axis=1)
    number = jnp.arange(1, NR + 1, dtype=jnp.int32)[None, :, None]
    ours = row * 2 + jnp.arange(2, dtype=jnp.int32)
    own = jnp.sum(jnp.where(slots[:, :, None] == ours, number, 0), axis=1) - 1
    rel = jnp.array([0, 3, 1, 2, 0, 3, 1, 0, 3, 1, 2, 0, 3, 1, 2, 2], jnp.int32)
    flip = jnp.array([0, 0, 0, 0, 1, 1, 1, 0, 0, 0, 0, 1, 1, 1, 1, 1], jnp.int32)
    cross = jnp.array([0, 0, 0, 0, 0, 0, 0, 1, 1, 1, 1, 1, 1, 1, 0, 1], jnp.int32)
    cs = (core + cross) % 2
    place = ((((y + rel * (1 + 2 * cs)) % 4) * 2 + (h + flip) % 2) * 2 + cs) * 16
    place = place.astype(jnp.int32)

    s, l = sigma_anc, lower_blocks
    p1 = z_first(s)
    p2 = z_second(s)
    sw = swap_w(s)
    wa = sw[:, :3 * B]
    q1 = y_first(l)
    q2 = y_second(l)
    p1, q1, q2 = tie(p1, q1, q2)
    p3 = z_first(p1)
    lh = swap_h(l)
    q3 = y_first(q1)
    p2, p3, wa, lh, q3 = tie(p2, p3, wa, lh, q3)
    a1 = z_first(wa)
    a2 = z_second(wa)
    far = swap_w(jnp.stack([v[:, 3 * B:] for v in (p1, p2, p3)]))
    r1 = y_first(lh)
    r2 = y_second(lh)
    r1, r2, q1, q3 = tie(r1, r2, q1, q3)
    r3 = y_first(r1)
    x0 = jnp.stack([l, q1])
    x1 = jnp.stack([q2, q3])
    tx0 = swap_core(x0)
    tx1 = swap_core(x1)
    t0 = swap_core(lh)
    t2 = swap_core(jnp.stack([r1, r2]))
    a1, a2, far = tie(a1, a2, far)
    a3 = z_first(a1)
    t3 = swap_core(r3)
    s, p1, p2, p3, sw, a1, a2, far = in_hbm(s, p1, p2, p3, sw, a1, a2, far)
    a3 = pltpu.with_memory_space_constraint(a3, pltpu.VMEM)
    lh, r1, r2, x0, x1 = in_hbm(lh, r1, r2, x0, x1)
    t0, tx0, tx1, t2 = in_hbm(t0, tx0, tx1, t2)
    r3, t3 = [pltpu.with_memory_space_constraint(v, pltpu.VMEM) for v in (r3, t3)]

    hbm = pl.BlockSpec(memory_space=pltpu.HBM)
    smem = pl.BlockSpec(memory_space=pltpu.SMEM)
    vmem = pl.BlockSpec(memory_space=pltpu.VMEM)
    params = pltpu.CompilerParams(vmem_limit_bytes=VMEM_LIMIT)
    panel_shape = pltpu.VMEM((SUP, NR, B, B), jnp.bfloat16)
    held_shape = pltpu.VMEM((NA, ROWS, B), jnp.bfloat16)
    acc_shape = pltpu.VMEM((SUP, ROWS, B), jnp.float32)
    held = pl.pallas_call(
        hold_kernel,
        out_shape=held_shape,
        in_specs=[hbm] * 8,
        out_specs=vmem,
        scratch_shapes=[pltpu.SemaphoreType.DMA((29,))],
        compiler_params=params,
    )(s, p1, p2, p3, sw, a1, a2, far)
    blocks = pl.pallas_call(
        panel_kernel,
        out_shape=panel_shape,
        in_specs=[smem] + [hbm] * 9,
        out_specs=vmem,
        scratch_shapes=[pltpu.SemaphoreType.DMA((14,))],
        compiler_params=params,
    )(place, x0, x1, lh, r1, r2, tx0, tx1, t0, t2)
    held, blocks = [pltpu.with_memory_space_constraint(v, pltpu.VMEM) for v in (held, blocks)]
    blocks, acc = pl.pallas_call(
        main_kernel,
        out_shape=(panel_shape, acc_shape),
        in_specs=[smem] * 3 + [vmem] * 4,
        out_specs=(vmem, vmem),
        input_output_aliases={4: 0},
        scratch_shapes=[pltpu.SemaphoreType.DMA((2,))],
        compiler_params=params,
    )(sorted_slots, sorted_blocks, place, held, blocks, r3, t3)
    blocks, acc = [pltpu.with_memory_space_constraint(v, pltpu.VMEM) for v in (blocks, acc)]
    sigma_off, keep, send, _ = pl.pallas_call(
        late_kernel,
        out_shape=(
            jax.ShapeDtypeStruct((ROWS, SUP * B), jnp.bfloat16),
            jax.ShapeDtypeStruct((8, SUP, 16, B), jnp.float32),
            jax.ShapeDtypeStruct((8, SUP, 16, B), jnp.bfloat16),
            held_shape,
        ),
        in_specs=[smem] * 4 + [vmem] * 4,
        out_specs=(hbm,) + (vmem,) * 3,
        input_output_aliases={4: 3},
        scratch_shapes=[
            pltpu.VMEM((SUP, ROWS, B), jnp.float32),
            pltpu.VMEM((SUP, ROWS, B), jnp.bfloat16),
            pltpu.SemaphoreType.DMA((SUP,)),
        ],
        compiler_params=params,
    )(sorted_slots, sorted_blocks, own, core.reshape(1).astype(jnp.int32), held, blocks, acc, a3)

    one = (keep + swap_core(send).astype(jnp.float32)).reshape(4, 2, SUP, 16, B)
    kept = lax.dynamic_index_in_dim(one, h, 1, keepdims=False)
    sent = lax.dynamic_index_in_dim(one, 1 - h, 1, keepdims=False).astype(jnp.bfloat16)
    two = kept + swap_h(sent).astype(jnp.float32)
    narrow = two.astype(jnp.bfloat16)
    parts = [move_y(lax.dynamic_index_in_dim(narrow, (y + step) % 4, 0, keepdims=False), step) for step in (2, 1, -1)]
    total = lax.dynamic_index_in_dim(two, y, 0, keepdims=False)
    for part in parts:
        total = total + part.astype(jnp.float32)
    return sigma_off, inv_diag - total


def solution(mesh):
    in_specs = (P("prow", "pcol"), P("pcol", None, "prow", None), P(), P(), P("pcol", "prow", None))
    out_specs = (P("prow", "pcol"), P("pcol", "prow", None))
    return jax.shard_map(
        per_device, mesh=mesh, in_specs=in_specs, out_specs=out_specs, check_vma=False
    )
```

```python
import jax
import jax.numpy as jnp
from jax import lax
from jax.experimental import pallas as pl
from jax.experimental.pallas import tpu as pltpu
from jax.sharding import PartitionSpec as P

B = 256
NR = 16
SUP = 4
NA = 32
EARLY = 13
ROWS = 2 * B
VMEM_LIMIT = 16 * 1024 * 1024
AXES = ("prow", "pcol")


def permute(x, fn):
    pairs = []
    for y in range(4):
        for h in range(2):
            for co in range(2):
                for z in range(4):
                    for w in range(2):
                        ty, th, tc, tz, tw = fn(y, h, co, z, w)
                        target = ((ty % 4) * 4 + (th % 2) * 2 + tc % 2) * 8 + (tz % 4) * 2 + tw % 2
                        pairs.append(((y * 4 + h * 2 + co) * 8 + z * 2 + w, target))
    return lax.ppermute(x, AXES, pairs)


def z_first(x):
    return permute(x, lambda y, h, co, z, w: (y, h, co, z + 1 - 2 * co, w))


def z_second(x):
    return permute(x, lambda y, h, co, z, w: (y, h, co, z - 1 + 2 * co, w))


def y_first(x):
    return permute(x, lambda y, h, co, z, w: (y + 1 - 2 * co, h, co, z, w))


def y_second(x):
    return permute(x, lambda y, h, co, z, w: (y - 1 + 2 * co, h, co, z, w))


def move_y(x, step):
    return permute(x, lambda y, h, co, z, w: (y + step, h, co, z, w))


def swap_h(x):
    return permute(x, lambda y, h, co, z, w: (y, h + 1, co, z, w))


def swap_core(x):
    return permute(x, lambda y, h, co, z, w: (y, h, co + 1, z, w))


def swap_w(x):
    return permute(x, lambda y, h, co, z, w: (y, h, co, z, w + 1))


def tie(*arrays):
    return lax.optimization_barrier(arrays)


def in_hbm(*arrays):
    return [pltpu.with_memory_space_constraint(v, pltpu.HBM) for v in arrays]


def start_wait(copies):
    for copy in copies:
        copy.start()
    for copy in copies:
        copy.wait()


def slot_copies(parts, sv, sem):
    return [pltpu.make_async_copy(part, sv.at[n], sem.at[n]) for n, part in enumerate(parts)]


def columns(src, count):
    return [src.at[:, pl.ds(j * B, B)] for j in range(count)]


def hold_kernel(s, p1, p2, p3, sw, a1, a2, far, sv, done, sem):
    done[...] = jnp.zeros_like(done)
    parts = []
    for src in (s, p1, p2, p3, sw):
        parts += columns(src, 4)
    for i, src in enumerate((a1, a2)):
        parts += columns(src, 3) + [far.at[i]]
    start_wait(slot_copies(parts + [far.at[2]], sv, sem))


def row_copies(parts, first, place_ref, lv, sem):
    copies = []
    for n, part in enumerate(parts):
        row = pl.multiple_of(place_ref[first + n], 16)
        copies.append(pltpu.make_async_copy(part, lv.at[:, :, pl.ds(row, 16), :], sem.at[n]))
    return copies


def panel_kernel(place_ref, x0, x1, lh, r1, r2, tx0, tx1, t0, t2, lv, sem):
    parts = [x0.at[0], x0.at[1], x1.at[0], x1.at[1], lh, r1, r2]
    parts += [tx0.at[0], tx0.at[1], tx1.at[0], tx1.at[1], t0, t2.at[0], t2.at[1]]
    start_wait(row_copies(parts, 0, place_ref, lv, sem))


def product(slot_ref, block_ref, k, first, count, sv, lv):
    left = jnp.concatenate([sv[slot_ref[k, i]] for i in range(first, first + count)], axis=1)
    right = jnp.concatenate([lv[k, block_ref[k, i]] for i in range(first, first + count)], axis=0)
    return jnp.dot(left, right, preferred_element_type=jnp.float32)


def main_kernel(slot_ref, block_ref, place_ref, sv, lv_in, r3, t3, done, lv, acc, sem):
    start_wait(row_copies([r3, t3], 14, place_ref, lv, sem))
    for k in range(SUP):
        acc[k] = product(slot_ref, block_ref, k, 0, EARLY, sv, lv)


def late_kernel(slot_ref, block_ref, own_ref, core_ref, sv_in, lv, acc_in, a3, off_out, keep_out, send_out, sv,
                acc, off_ref, sem):
    for j in range(3):
        sv[29 + j] = a3[:, j * B:(j + 1) * B]
    stores = []
    core = core_ref[0]
    for k in range(SUP):
        acc[k] = acc_in[k] + product(slot_ref, block_ref, k, EARLY, NR - EARLY, sv, lv)
    for k in range(SUP):
        offs, owns = [], []
        for t in range(2):
            c = own_ref[k, t]
            alive = (c >= 0).astype(jnp.float32)
            off = (acc[k, pl.ds(t * B, B)] * -alive).astype(jnp.bfloat16)
            off_ref[k, pl.ds(t * B, B)] = off
            offs.append(off)
            owns.append(lv[k, jnp.maximum(c, 0)])
        stores.append(pltpu.make_async_copy(off_ref.at[k], off_out.at[:, pl.ds(k * B, B)], sem.at[k]))
        stores[-1].start()
        total = lax.dot_general(jnp.concatenate(owns, axis=0), jnp.concatenate(offs, axis=0),
                                (((0,), (0,)), ((), ())), preferred_element_type=jnp.float32)
        part = (0.5 * (total + total.T)).reshape(8, 2, 16, B)
        keep_out[:, k] = jnp.where(core == 0, part[:, 0], part[:, 1])
        send_out[:, k] = jnp.where(core == 0, part[:, 1], part[:, 0]).astype(jnp.bfloat16)
    for store in stores:
        store.wait()


def per_device(sigma_anc, lower_blocks, row_blocks, slot_of, inv_diag):
    row = lax.axis_index("prow")
    col = lax.axis_index("pcol")
    y, h, core = row // 4, (row // 2) % 2, row % 2
    z, w = col // 2, col % 2

    my_rows = lax.dynamic_slice_in_dim(row_blocks, col * SUP, SUP, 0)
    order = jnp.arange(NA, dtype=jnp.int32)
    slots = jnp.sum(jnp.where(my_rows[:, :, None] == order, slot_of, 0), axis=2)
    sc = slots // 4
    dz = (sc // 2 - z) % 4
    one_away = jnp.where(dz == 3, 1 + core, 2 - core)
    group = jnp.where(dz == 0, 0, jnp.where(dz == 2, 3, one_away))
    near = group * 4 + slots % 4
    far = jnp.where(group == 3, jnp.where(slots % 4 == 3, 28, 29 + slots % 4), 16 + group * 4 + slots % 4)
    pos = jnp.where(sc % 2 == w, near, far).astype(jnp.int32)
    rank = jnp.sum((pos[:, None, :] < pos[:, :, None]).astype(jnp.int32), axis=2)
    ranked = rank[:, :, None] == jnp.arange(NR, dtype=jnp.int32)
    index = jnp.arange(NR, dtype=jnp.int32)[None, :, None]
    sorted_slots = jnp.sum(jnp.where(ranked, pos[:, :, None], 0), axis=1)
    sorted_blocks = jnp.sum(jnp.where(ranked, index, 0), axis=1)
    number = jnp.arange(1, NR + 1, dtype=jnp.int32)[None, :, None]
    ours = row * 2 + jnp.arange(2, dtype=jnp.int32)
    own = jnp.sum(jnp.where(slots[:, :, None] == ours, number, 0), axis=1) - 1
    rel = jnp.array([0, 3, 1, 2, 0, 3, 1, 0, 3, 1, 2, 0, 3, 1, 2, 2], jnp.int32)
    flip = jnp.array([0, 0, 0, 0, 1, 1, 1, 0, 0, 0, 0, 1, 1, 1, 1, 1], jnp.int32)
    cross = jnp.array([0, 0, 0, 0, 0, 0, 0, 1, 1, 1, 1, 1, 1, 1, 0, 1], jnp.int32)
    cs = (core + cross) % 2
    place = ((((y + rel * (1 + 2 * cs)) % 4) * 2 + (h + flip) % 2) * 2 + cs) * 16
    place = place.astype(jnp.int32)

    s, l = sigma_anc, lower_blocks
    p1 = z_first(s)
    p2 = z_second(s)
    sw = swap_w(s)
    wa = sw[:, :3 * B]
    q1 = y_first(l)
    q2 = y_second(l)
    p1, q1, q2 = tie(p1, q1, q2)
    p3 = z_first(p1)
    lh = swap_h(l)
    q3 = y_first(q1)
    p2, p3, wa, lh, q3 = tie(p2, p3, wa, lh, q3)
    a1 = z_first(wa)
    a2 = z_second(wa)
    far = swap_w(jnp.stack([v[:, 3 * B:] for v in (p1, p2, p3)]))
    r1 = y_first(lh)
    r2 = y_second(lh)
    r1, r2, q1, q3 = tie(r1, r2, q1, q3)
    r3 = y_first(r1)
    x0 = jnp.stack([l, q1])
    x1 = jnp.stack([q2, q3])
    tx0 = swap_core(x0)
    tx1 = swap_core(x1)
    t0 = swap_core(lh)
    t2 = swap_core(jnp.stack([r1, r2]))
    a1, a2, far = tie(a1, a2, far)
    a3 = z_first(a1)
    s, p1, p2, p3, sw = in_hbm(s, p1, p2, p3, sw)
    a1, a2, far = [pltpu.with_memory_space_constraint(v, pltpu.VMEM) for v in (a1, a2, far)]
    a3 = pltpu.with_memory_space_constraint(a3, pltpu.VMEM)
    hbm = pl.BlockSpec(memory_space=pltpu.HBM)
    smem = pl.BlockSpec(memory_space=pltpu.SMEM)
    vmem = pl.BlockSpec(memory_space=pltpu.VMEM)
    params = pltpu.CompilerParams(vmem_limit_bytes=VMEM_LIMIT)
    panel_shape = pltpu.VMEM((SUP, NR, B, B), jnp.bfloat16)
    held_shape = pltpu.VMEM((NA, ROWS, B), jnp.bfloat16)
    acc_shape = pltpu.VMEM((SUP, ROWS, B), jnp.float32)
    held, done = pl.pallas_call(
        hold_kernel,
        out_shape=(held_shape, jax.ShapeDtypeStruct((8, 128), jnp.float32)),
        in_specs=[hbm] * 5 + [vmem] * 3,
        out_specs=(vmem, vmem),
        scratch_shapes=[pltpu.SemaphoreType.DMA((29,))],
        compiler_params=params,
    )(s, p1, p2, p3, sw, a1, a2, far)
    r3, done = tie(r3, done)
    t3 = swap_core(r3)
    lh, r1, r2, x0, x1 = in_hbm(lh, r1, r2, x0, x1)
    t0, tx0, tx1, t2 = in_hbm(t0, tx0, tx1, t2)
    r3, t3 = [pltpu.with_memory_space_constraint(v, pltpu.VMEM) for v in (r3, t3)]

    blocks = pl.pallas_call(
        panel_kernel,
        out_shape=panel_shape,
        in_specs=[smem] + [hbm] * 9,
        out_specs=vmem,
        scratch_shapes=[pltpu.SemaphoreType.DMA((14,))],
        compiler_params=params,
    )(place, x0, x1, lh, r1, r2, tx0, tx1, t0, t2)
    held, blocks = [pltpu.with_memory_space_constraint(v, pltpu.VMEM) for v in (held, blocks)]
    blocks, acc = pl.pallas_call(
        main_kernel,
        out_shape=(panel_shape, acc_shape),
        in_specs=[smem] * 3 + [vmem] * 5,
        out_specs=(vmem, vmem),
        input_output_aliases={4: 0},
        scratch_shapes=[pltpu.SemaphoreType.DMA((2,))],
        compiler_params=params,
    )(sorted_slots, sorted_blocks, place, held, blocks, r3, t3, done)
    blocks, acc = [pltpu.with_memory_space_constraint(v, pltpu.VMEM) for v in (blocks, acc)]
    sigma_off, keep, send, _ = pl.pallas_call(
        late_kernel,
        out_shape=(
            jax.ShapeDtypeStruct((ROWS, SUP * B), jnp.bfloat16),
            jax.ShapeDtypeStruct((8, SUP, 16, B), jnp.float32),
            jax.ShapeDtypeStruct((8, SUP, 16, B), jnp.bfloat16),
            held_shape,
        ),
        in_specs=[smem] * 4 + [vmem] * 4,
        out_specs=(hbm,) + (vmem,) * 3,
        input_output_aliases={4: 3},
        scratch_shapes=[
            pltpu.VMEM((SUP, ROWS, B), jnp.float32),
            pltpu.VMEM((SUP, ROWS, B), jnp.bfloat16),
            pltpu.SemaphoreType.DMA((SUP,)),
        ],
        compiler_params=params,
    )(sorted_slots, sorted_blocks, own, core.reshape(1).astype(jnp.int32), held, blocks, acc, a3)

    halves = (keep + swap_core(send).astype(jnp.float32)).astype(jnp.bfloat16)
    parts = lax.all_to_all(halves, "prow", split_axis=0, concat_axis=0, tiled=True,
                           axis_index_groups=[list(range(c, 16, 2)) for c in range(2)])
    total = jnp.sum(parts.astype(jnp.float32), axis=0)
    return sigma_off, inv_diag - total


def solution(mesh):
    in_specs = (P("prow", "pcol"), P("pcol", None, "prow", None), P(), P(), P("pcol", "prow", None))
    out_specs = (P("prow", "pcol"), P("pcol", "prow", None))
    return jax.shard_map(
        per_device, mesh=mesh, in_specs=in_specs, out_specs=out_specs, check_vma=False
    )
```
